128 devices in a mesh: row: 16 (over z, x_lo, core), chan: 8 (over x_hi, y).
Axes of the slice: x: 4 (x_hi: 2, x_lo: 2; x = x_hi * 2 + x_lo), y: 4, z: 4, core: 2. Of those that a mesh axis runs over, the one named last changes fastest.
Arguments:
- pair: bfloat16 [2048, 2048, 128], P('row', 'chan'), may hold values from -6 to 6
- token_mask: int32 [2048], replicated, may hold values 0 or 1
- w_left: bfloat16 [128, 256], replicated, may hold values from -0.5 to 0.5
- w_right: bfloat16 [128, 256], replicated, may hold values from -0.5 to 0.5
- w_gate: bfloat16 [128, 128], replicated, may hold values from -0.5 to 0.5
- w_out: bfloat16 [128, 128], replicated, may hold values from -0.5 to 0.5
- out_gain: float32 [128], replicated, may hold values from 0.1 to 1.9
Outputs:
- update: bfloat16 [2048, 512, 128], P('row', 'chan')
The draws below stay inside these ranges and needn't reach their ends.
All inputs are finite; a program needn't handle non-finite values.
Results may differ from the reference program's by a relative error of at most 0.019.
Values may be sent and summed in bfloat16 or wider, within the bound.
No kernel may reach another device: no remote copies, remote signals or barrier semaphores. Data moves between devices by JAX's collectives and lax.ppermute only.
A program may use at most 256 MiB of HBM per device.

```python
import jax
import jax.numpy as jnp
from jax import lax

C = 128
TOK_ROW = 128
WIN_BLK = 32
TOKENS = 2048
WIN = 512
N_ROW = 16


def with_ends(entries, rng, low, high):
    shape = entries.shape
    spot = [jax.random.randint(jax.random.fold_in(rng, axis), (), 0, shape[axis]) for axis in range(len(shape))]
    entries = entries.at[tuple(spot)].set(low)
    longest = shape.index(max(shape))
    spot[longest] = (spot[longest] + 1) % shape[longest]
    return entries.at[tuple(spot)].set(high)


def steps_of(stream_key, dims, shards, low, high):
    loudness = 1.0
    for dim, shards_of in shards:
        draws = jax.random.uniform(jax.random.fold_in(jax.random.fold_in(stream_key, 6), dim), (shards_of,), jnp.float32, low / len(shards), high / len(shards))
        loudness = loudness * jnp.repeat(jnp.exp(draws), dims[dim] // shards_of).reshape((-1,) + (1,) * (len(dims) - 1 - dim))
    return loudness


def scatter_about(key, shape, spread, reach, cuts=(), held_as=jnp.bfloat16):
    entries = jax.random.normal(key, shape, jnp.float32) * spread
    if len(cuts) > 0:
        entries = steps_of(key, shape, cuts, -0.22, 0.18) * entries
    return jnp.clip(entries, min=-reach, max=reach).astype(held_as)


def setup_inputs(seed: int = 0) -> dict:
    key_of = jax.random.split(jax.random.key(seed), 8)
    return {
        "pair": scatter_about(key_of[0], (TOKENS, TOKENS, C), 1.0, 6.0, ((0, 16), (1, 8))),
        "token_mask": with_ends((jax.random.randint(key_of[1], (TOKENS,), 0, 8) < 7).astype(jnp.int32), jax.random.fold_in(key_of[1], 1), 0, 1),
        "w_left": scatter_about(key_of[2], (C, 2 * C), C ** -0.5, 0.5),
        "w_right": scatter_about(key_of[3], (C, 2 * C), C ** -0.5, 0.5),
        "w_gate": scatter_about(key_of[4], (C, C), C ** -0.5, 0.5),
        "w_out": scatter_about(key_of[5], (C, C), C ** -0.5, 0.5),
        "out_gain": jnp.clip(1.0 + 0.18 * jax.random.normal(key_of[6], (C,), jnp.float32), 0.1, 1.9),
    }


def layer_norm(values):
    mean = lax.optimization_barrier(jnp.mean(values, axis=-1, keepdims=True))
    centred = values - mean
    var = lax.optimization_barrier(jnp.mean(centred * centred, axis=-1, keepdims=True))
    return centred * lax.rsqrt(var + 1e-05)

def project(normed, row_mask, col_mask, weight):
    rows, cols, chans = normed.shape
    both = jnp.dot(normed.reshape(rows * cols, chans), weight, preferred_element_type=jnp.float32)
    both = both.reshape(rows, cols, 2 * chans)
    gated = jax.nn.sigmoid(both[:, :, :chans]) * both[:, :, chans:]
    gated = gated * row_mask[:, None, None] * col_mask[None, :, None]
    return gated.astype(jnp.bfloat16)

def reference(pair, token_mask, w_left, w_right, w_gate, w_out, out_gain):
    maskf = token_mask.astype(jnp.float32)
    blocks = pair.reshape(N_ROW, TOK_ROW, TOKENS, C)
    mask_blocks = maskf.reshape(N_ROW, TOK_ROW)
    win_rows = blocks[:, :WIN_BLK].reshape(WIN, TOKENS, C)
    win_mask = mask_blocks[:, :WIN_BLK].reshape(WIN)
    win_normed = layer_norm(win_rows.astype(jnp.float32)).astype(jnp.bfloat16)
    right = project(win_normed, win_mask, maskf, w_right).astype(jnp.float32)

    def one_block(inputs):
        block, block_mask = inputs
        normed = layer_norm(block.astype(jnp.float32)).astype(jnp.bfloat16)
        left = project(normed, block_mask, maskf, w_left).astype(jnp.float32)
        product = jnp.einsum('ikc,jkc->ijc', left, right).astype(jnp.bfloat16)
        normed_product = (layer_norm(product.astype(jnp.float32)) * out_gain).astype(jnp.bfloat16)
        gate_in = normed.reshape(TOK_ROW, N_ROW, TOK_ROW, C)[:, :, :WIN_BLK].reshape(TOK_ROW * WIN, C)
        gate = jnp.dot(gate_in, w_gate, preferred_element_type=jnp.float32)
        outcome = jnp.dot(normed_product.reshape(TOK_ROW * WIN, C), w_out, preferred_element_type=jnp.float32)
        return (jax.nn.sigmoid(gate) * outcome).astype(jnp.bfloat16).reshape(TOK_ROW, WIN, C)
    result = lax.map(one_block, (blocks, mask_blocks))
    return result.reshape(TOKENS, WIN, C)
```

```python
import functools

import jax
import jax.numpy as jnp
from jax import lax
from jax.experimental import pallas as pl
from jax.experimental.pallas import tpu as pltpu
from jax.sharding import PartitionSpec as P

WIN_BLK = 32
ROW_STEP = 16
AXES = ("row", "chan")
NT = (((1,), (1,)), ((), ()))
TN = (((0,), (0,)), ((), ()))


def normed_rows(x):
    chans = x.shape[-1]
    avg = jnp.full((chans, chans), 1.0 / chans, jnp.bfloat16)
    mean = jnp.dot(x, avg, preferred_element_type=jnp.float32)
    centred = x.astype(jnp.float32) - mean
    var = jnp.dot((centred * centred).astype(jnp.bfloat16), avg, preferred_element_type=jnp.float32)
    return (centred * lax.rsqrt(var + 1e-05)).astype(jnp.bfloat16)


def project_kernel(x_ref, w_ref, mask_ref, o_ref, swap):
    rows, cols, chans = x_ref.shape
    normed = normed_rows(x_ref[...].reshape(rows * cols, chans))
    for i in range(rows):
        both = lax.dot_general(w_ref[...], normed[i * cols:(i + 1) * cols], NT, preferred_element_type=jnp.float32)
        gated = (jnp.tanh(both[:chans]) + 1.0) * both[chans:] * mask_ref[i:i + 1, :]
        for h in range(cols // 128):
            swap[h, i * chans:(i + 1) * chans, :] = gated[:, h * 128:(h + 1) * 128]
    for c in range(chans):
        for h in range(cols // 128):
            o_ref[c, :, h * 128:(h + 1) * 128] = swap[h, pl.ds(c, rows, stride=chans), :].astype(jnp.bfloat16)


def project(pair, weight, mask, first, rows):
    cols, chans = pair.shape[1:]
    weight = (0.5 * weight.T).astype(jnp.bfloat16)
    base = first // ROW_STEP
    return pl.pallas_call(
        project_kernel,
        grid=(rows // ROW_STEP,),
        in_specs=[
            pl.BlockSpec((ROW_STEP, cols, chans), lambda s: (base + s, 0, 0)),
            pl.BlockSpec((2 * chans, chans), lambda s: (0, 0)),
            pl.BlockSpec((ROW_STEP, cols), lambda s: (base + s, 0)),
        ],
        out_specs=pl.BlockSpec((chans, ROW_STEP, cols), lambda s: (0, s, 0)),
        out_shape=jax.ShapeDtypeStruct((chans, rows, cols), jnp.bfloat16),
        scratch_shapes=[pltpu.VMEM((cols // 128, ROW_STEP * chans, 128), jnp.float32)],
        compiler_params=pltpu.CompilerParams(vmem_limit_bytes=48 << 20),
    )(pair, weight, mask)


def gate_kernel(x_ref, w_ref, o_ref):
    rows, blks, blk, _, chans = x_ref.shape[0], x_ref.shape[1], WIN_BLK, 0, x_ref.shape[-1]
    normed = normed_rows(x_ref[...].reshape(rows * blks * blk, chans))
    gate = jnp.dot(normed, w_ref[...], preferred_element_type=jnp.float32)
    o_ref[...] = (0.5 * jnp.tanh(gate) + 0.5).reshape(rows, blks * blk, chans).astype(jnp.bfloat16)


def gate_of(pair, w_gate):
    rows, cols, chans = pair.shape
    blks = cols // 128
    blocks = pair.reshape(rows, blks, 128, chans)
    return pl.pallas_call(
        gate_kernel,
        grid=(rows // 32,),
        in_specs=[
            pl.BlockSpec((32, blks, WIN_BLK, chans), lambda s: (s, 0, 0, 0)),
            pl.BlockSpec((chans, chans), lambda s: (0, 0)),
        ],
        out_specs=pl.BlockSpec((32, blks * WIN_BLK, chans), lambda s: (s, 0, 0)),
        out_shape=jax.ShapeDtypeStruct((rows, blks * WIN_BLK, chans), jnp.bfloat16),
        compiler_params=pltpu.CompilerParams(vmem_limit_bytes=48 << 20),
    )(blocks, (0.5 * w_gate).astype(jnp.bfloat16))


def product_kernel(a_ref, b_ref, o_ref, acc):
    steps, parts, rows, depth = a_ref.shape
    wins, blk = b_ref.shape[0], b_ref.shape[2]
    half = rows // 2
    for q in range(parts):
        term = lax.dot_general(
            a_ref[:, q].reshape(steps * rows, depth), b_ref[:, q].reshape(wins * blk, depth), NT,
            preferred_element_type=jnp.float32)
        if q == 0:
            acc[...] = term
        else:
            acc[...] += term
    low = lax.broadcasted_iota(jnp.int32, (half, 128), 1) < 64
    for r in range(steps):
        for m in range(wins * blk // 128):
            top = acc[r * rows:r * rows + half, m * 128:(m + 1) * 128]
            bot = acc[r * rows + half:(r + 1) * rows, m * 128:(m + 1) * 128]
            o_ref[r, 2 * m] = jnp.where(low, top, pltpu.roll(bot, 64, 1)).astype(jnp.bfloat16)
            o_ref[r, 2 * m + 1] = jnp.where(low, pltpu.roll(top, 64, 1), bot).astype(jnp.bfloat16)


def product_of(left, right, n_row, n_chan):
    rows, depth = left.shape[1:]
    blk = right.shape[1]
    left = left.reshape(n_row, n_chan, rows, depth)
    right = right.reshape(n_row, n_chan, blk, depth)
    steps = 4
    out = pl.pallas_call(
        product_kernel,
        grid=(n_row // steps,),
        in_specs=[
            pl.BlockSpec((steps, n_chan, rows, depth), lambda s: (s, 0, 0, 0)),
            pl.BlockSpec((n_row, n_chan, blk, depth), lambda s: (0, 0, 0, 0)),
        ],
        out_specs=pl.BlockSpec((steps, n_chan, rows // 2, 128), lambda s: (s, 0, 0, 0)),
        out_shape=jax.ShapeDtypeStruct((n_row, n_chan, rows // 2, 128), jnp.bfloat16),
        scratch_shapes=[pltpu.VMEM((steps * rows, n_row * blk), jnp.float32)],
        compiler_params=pltpu.CompilerParams(vmem_limit_bytes=48 << 20),
    )(left, right)
    return out.reshape(n_row * n_chan, rows // 2, 128)


def finish_kernel(p_ref, gain_ref, w_ref, gate_ref, o_ref, swap):
    chans, subs, lanes = p_ref.shape
    x = p_ref[...].astype(jnp.float32)
    mean = jnp.sum(x, axis=0) * (1.0 / chans)
    centred = x - mean[None]
    var = jnp.sum(centred * centred, axis=0) * (1.0 / chans)
    swap[...] = (centred * lax.rsqrt(var + 1e-05)[None]).reshape(chans * subs, lanes)
    half = lanes // 2
    for s in range(subs):
        normed = (swap[pl.ds(s, chans, stride=subs), :] * gain_ref[...]).astype(jnp.bfloat16)
        outcome = lax.dot_general(normed, w_ref[...], TN, preferred_element_type=jnp.float32)
        for h in range(2):
            gate = gate_ref[h, s].astype(jnp.float32)
            o_ref[h, s] = (gate * outcome[h * half:(h + 1) * half]).astype(jnp.bfloat16)


def finish(product, out_gain, w_out, gate):
    chans, subs, lanes = product.shape
    rows, wins = gate.shape[:2]
    step = 16
    out = pl.pallas_call(
        finish_kernel,
        grid=(subs // step,),
        in_specs=[
            pl.BlockSpec((chans, step, lanes), lambda s: (0, s, 0)),
            pl.BlockSpec((chans, 1), lambda s: (0, 0)),
            pl.BlockSpec((chans, chans), lambda s: (0, 0)),
            pl.BlockSpec((2, step, wins, chans), lambda s: (0, s, 0, 0)),
        ],
        out_specs=pl.BlockSpec((2, step, wins, chans), lambda s: (0, s, 0, 0)),
        out_shape=jax.ShapeDtypeStruct((2, subs, wins, chans), jnp.bfloat16),
        scratch_shapes=[pltpu.VMEM((chans * step, lanes), jnp.float32)],
        compiler_params=pltpu.CompilerParams(vmem_limit_bytes=48 << 20),
    )(product, out_gain.reshape(chans, 1), w_out, gate.reshape(2, subs, wins, chans))
    return out.reshape(rows, wins, chans)


def spread(values):
    return lax.all_to_all(values, AXES, split_axis=0, concat_axis=0, tiled=True)


def per_device(n_row, n_chan, pair, token_mask, w_left, w_right, w_gate, w_out, out_gain):
    tok_rows, columns, chans = pair.shape
    maskf = token_mask.astype(jnp.float32)
    row_mask = lax.dynamic_slice_in_dim(maskf, lax.axis_index("row") * tok_rows, tok_rows, 0)
    col_mask = lax.dynamic_slice_in_dim(maskf, lax.axis_index("chan") * columns, columns, 0)
    mask = row_mask[:, None] * col_mask[None, :]
    right = spread(project(pair, w_right, mask, 0, WIN_BLK))
    left = spread(project(pair, w_left, mask, 0, tok_rows))
    gate = gate_of(pair, w_gate)
    product = spread(product_of(left, right, n_row, n_chan))
    return finish(product, out_gain, w_out, gate)


def solution(mesh):
    in_specs = (P("row", "chan", None), P(), P(), P(), P(), P(), P())
    out_specs = P("row", "chan", None)
    body = functools.partial(per_device, mesh.shape["row"], mesh.shape["chan"])
    return jax.shard_map(
        body, mesh=mesh, in_specs=in_specs, out_specs=out_specs, check_vma=False
    )
```

```python
import jax
import jax.numpy as jnp
from jax import lax
from jax.experimental import pallas as pl
from jax.experimental.pallas import tpu as pltpu
from jax.sharding import Mesh, PartitionSpec as P

WIN_BLK = 32
ROW_STEP = 16
N_ROW = 16
ROW = ("z", "x_lo", "core")
CHAN = ("x_hi", "y")
PLANE = ("x_lo", "core", "x_hi", "y")
NT = (((1,), (1,)), ((), ()))
TN = (((0,), (0,)), ((), ()))


def normed_rows(x):
    chans = x.shape[-1]
    avg = jnp.full((chans, chans), 1.0 / chans, jnp.bfloat16)
    mean = jnp.dot(x, avg, preferred_element_type=jnp.float32)
    centred = x.astype(jnp.float32) - mean
    var = jnp.dot((centred * centred).astype(jnp.bfloat16), avg, preferred_element_type=jnp.float32)
    return (centred * lax.rsqrt(var + 1e-05)).astype(jnp.bfloat16)


def project_kernel(x_ref, w_ref, mask_ref, o_ref, swap):
    rows, cols, chans = x_ref.shape
    normed = normed_rows(x_ref[...].reshape(rows * cols, chans))
    for i in range(rows):
        both = lax.dot_general(w_ref[...], normed[i * cols:(i + 1) * cols], NT, preferred_element_type=jnp.float32)
        gated = (jnp.tanh(both[:chans]) + 1.0) * both[chans:] * mask_ref[i:i + 1, :]
        for h in range(cols // 128):
            swap[h, i * chans:(i + 1) * chans, :] = gated[:, h * 128:(h + 1) * 128]
    for c in range(chans):
        for h in range(cols // 128):
            o_ref[c, :, h * 128:(h + 1) * 128] = swap[h, pl.ds(c, rows, stride=chans), :].astype(jnp.bfloat16)


def project(pair, weight, mask, first, rows):
    cols, chans = pair.shape[1:]
    weight = (0.5 * weight.T).astype(jnp.bfloat16)
    base = first // ROW_STEP
    return pl.pallas_call(
        project_kernel,
        grid=(rows // ROW_STEP,),
        in_specs=[
            pl.BlockSpec((ROW_STEP, cols, chans), lambda s: (base + s, 0, 0)),
            pl.BlockSpec((2 * chans, chans), lambda s: (0, 0)),
            pl.BlockSpec((ROW_STEP, cols), lambda s: (base + s, 0)),
        ],
        out_specs=pl.BlockSpec((chans, ROW_STEP, cols), lambda s: (0, s, 0)),
        out_shape=jax.ShapeDtypeStruct((chans, rows, cols), jnp.bfloat16),
        scratch_shapes=[pltpu.VMEM((cols // 128, ROW_STEP * chans, 128), jnp.float32)],
        compiler_params=pltpu.CompilerParams(vmem_limit_bytes=48 << 20),
    )(pair, weight, mask)


def gate_kernel(x_ref, w_ref, o_ref):
    rows, blks, blk, _, chans = x_ref.shape[0], x_ref.shape[1], WIN_BLK, 0, x_ref.shape[-1]
    normed = normed_rows(x_ref[...].reshape(rows * blks * blk, chans))
    gate = jnp.dot(normed, w_ref[...], preferred_element_type=jnp.float32)
    o_ref[...] = (0.5 * jnp.tanh(gate) + 0.5).reshape(rows, blks * blk, chans).astype(jnp.bfloat16)


def gate_of(pair, w_gate):
    rows, cols, chans = pair.shape
    blks = cols // 128
    blocks = pair.reshape(rows, blks, 128, chans)
    return pl.pallas_call(
        gate_kernel,
        grid=(rows // 32,),
        in_specs=[
            pl.BlockSpec((32, blks, WIN_BLK, chans), lambda s: (s, 0, 0, 0)),
            pl.BlockSpec((chans, chans), lambda s: (0, 0)),
        ],
        out_specs=pl.BlockSpec((32, blks * WIN_BLK, chans), lambda s: (s, 0, 0)),
        out_shape=jax.ShapeDtypeStruct((rows, blks * WIN_BLK, chans), jnp.bfloat16),
        compiler_params=pltpu.CompilerParams(vmem_limit_bytes=48 << 20),
    )(blocks, (0.5 * w_gate).astype(jnp.bfloat16))


def product_kernel(a_ref, b_ref, o_ref, acc):
    steps, parts, rows, depth = a_ref.shape
    planes, per_plane, _, blk, _ = b_ref.shape
    wins = planes * per_plane * blk
    half = rows // 2
    for q in range(parts):
        term = lax.dot_general(
            a_ref[:, q].reshape(steps * rows, depth), b_ref[:, :, q].reshape(wins, depth), NT,
            preferred_element_type=jnp.float32)
        if q == 0:
            acc[...] = term
        else:
            acc[...] += term
    low = lax.broadcasted_iota(jnp.int32, (half, 128), 1) < 64
    for r in range(steps):
        for m in range(wins // 128):
            top = acc[r * rows:r * rows + half, m * 128:(m + 1) * 128]
            bot = acc[r * rows + half:(r + 1) * rows, m * 128:(m + 1) * 128]
            o_ref[r, 2 * m] = jnp.where(low, top, pltpu.roll(bot, 64, 1)).astype(jnp.bfloat16)
            o_ref[r, 2 * m + 1] = jnp.where(low, pltpu.roll(top, 64, 1), bot).astype(jnp.bfloat16)


def product_of(left, right, n_chan):
    rows, depth = left.shape[1:]
    planes, blk = right.shape[0], right.shape[2]
    steps = N_ROW // planes
    own = left.shape[0] // (steps * n_chan)
    left = left.reshape(steps, n_chan, own, rows, depth)
    right = right.reshape(planes, steps, n_chan, own, blk, depth)
    out = pl.pallas_call(
        product_kernel,
        grid=(own,),
        in_specs=[
            pl.BlockSpec((steps, n_chan, None, rows, depth), lambda c: (0, 0, c, 0, 0)),
            pl.BlockSpec((planes, steps, n_chan, None, blk, depth), lambda c: (0, 0, 0, c, 0, 0)),
        ],
        out_specs=pl.BlockSpec((steps, n_chan, None, rows // 2, 128), lambda c: (0, 0, c, 0, 0)),
        out_shape=jax.ShapeDtypeStruct((steps, n_chan, own, rows // 2, 128), jnp.bfloat16),
        scratch_shapes=[pltpu.VMEM((steps * rows, N_ROW * blk), jnp.float32)],
        compiler_params=pltpu.CompilerParams(vmem_limit_bytes=48 << 20),
    )(left, right)
    return out.reshape(-1, rows // 2, 128)


def finish_kernel(p_ref, gain_ref, w_ref, gate_ref, o_ref, swap):
    chans, subs, lanes = p_ref.shape
    x = p_ref[...].astype(jnp.float32)
    mean = jnp.sum(x, axis=0) * (1.0 / chans)
    centred = x - mean[None]
    var = jnp.sum(centred * centred, axis=0) * (1.0 / chans)
    swap[...] = (centred * lax.rsqrt(var + 1e-05)[None]).reshape(chans * subs, lanes)
    half = lanes // 2
    for s in range(subs):
        normed = (swap[pl.ds(s, chans, stride=subs), :] * gain_ref[...]).astype(jnp.bfloat16)
        outcome = lax.dot_general(normed, w_ref[...], TN, preferred_element_type=jnp.float32)
        for h in range(2):
            gate = gate_ref[h, s].astype(jnp.float32)
            o_ref[h, s] = (gate * outcome[h * half:(h + 1) * half]).astype(jnp.bfloat16)


def finish(product, out_gain, w_out, gate):
    chans, subs, lanes = product.shape
    rows, wins = gate.shape[:2]
    step = 16
    out = pl.pallas_call(
        finish_kernel,
        grid=(subs // step,),
        in_specs=[
            pl.BlockSpec((chans, step, lanes), lambda s: (0, s, 0)),
            pl.BlockSpec((chans, 1), lambda s: (0, 0)),
            pl.BlockSpec((chans, chans), lambda s: (0, 0)),
            pl.BlockSpec((2, step, wins, chans), lambda s: (0, s, 0, 0)),
        ],
        out_specs=pl.BlockSpec((2, step, wins, chans), lambda s: (0, s, 0, 0)),
        out_shape=jax.ShapeDtypeStruct((2, subs, wins, chans), jnp.bfloat16),
        scratch_shapes=[pltpu.VMEM((chans * step, lanes), jnp.float32)],
        compiler_params=pltpu.CompilerParams(vmem_limit_bytes=48 << 20),
    )(product, out_gain.reshape(chans, 1), w_out, gate.reshape(2, subs, wins, chans))
    return out.reshape(rows, wins, chans)


def spread(values):
    return lax.all_to_all(values, PLANE, split_axis=0, concat_axis=0, tiled=True)


def per_device(pair, token_mask, w_left, w_right, w_gate, w_out, out_gain):
    tok_rows, columns, chans = pair.shape
    maskf = token_mask.astype(jnp.float32)
    row_mask = lax.dynamic_slice_in_dim(maskf, lax.axis_index(ROW) * tok_rows, tok_rows, 0)
    col_mask = lax.dynamic_slice_in_dim(maskf, lax.axis_index(CHAN) * columns, columns, 0)
    mask = row_mask[:, None] * col_mask[None, :]
    right = spread(project(pair, w_right, mask, 0, WIN_BLK))
    left = project(pair, w_left, mask, 0, tok_rows)
    right, left = lax.optimization_barrier((right, left))
    right = lax.all_gather(right, "z", axis=0)
    left = spread(left)
    gate = gate_of(pair, w_gate)
    product = spread(product_of(left, right, maskf.shape[0] // columns))
    return finish(product, out_gain, w_out, gate)


def solution(mesh):
    by_axis = Mesh(mesh.devices.reshape(4, 2, 2, 2, 4), ROW + CHAN)
    in_specs = (P(ROW, CHAN, None), P(), P(), P(), P(), P(), P())
    out_specs = P(ROW, CHAN, None)
    return jax.shard_map(
        per_device, mesh=by_axis, in_specs=in_specs, out_specs=out_specs, check_vma=False
    )
```

```python
import functools

import jax
import jax.numpy as jnp
from jax import lax
from jax.experimental import pallas as pl
from jax.experimental.pallas import tpu as pltpu
from jax.sharding import PartitionSpec as P

TOK_ROW = 128
WIN_BLK = 32
ROW_STEP = 16
AXES = ("row", "chan")
NT = (((1,), (1,)), ((), ()))
TN = (((0,), (0,)), ((), ()))


def normed_rows(x):
    chans = x.shape[-1]
    avg = jnp.full((chans, chans), 1.0 / chans, jnp.bfloat16)
    mean = jnp.dot(x, avg, preferred_element_type=jnp.float32)
    centred = x.astype(jnp.float32) - mean
    var = jnp.dot((centred * centred).astype(jnp.bfloat16), avg, preferred_element_type=jnp.float32)
    return (centred * lax.rsqrt(var + 1e-05)).astype(jnp.bfloat16)


def project_kernel(first, tok_s_ref, tok_v_ref, x_ref, w_ref, o_ref, w_swap, swap):
    rows, cols, chans = x_ref.shape
    pitch = chans + 1

    @pl.when(pl.program_id(0) == 0)
    def _():
        w_swap[...] = (0.5 * w_ref[...].astype(jnp.float32)).T.astype(jnp.bfloat16)

    own_row = lax.axis_index("row") * TOK_ROW + first + pl.program_id(0) * rows
    own_col = lax.axis_index("chan") * (cols // 128)
    col_mask = [tok_v_ref[pl.ds(own_col + h, 1), :].astype(jnp.float32) for h in range(cols // 128)]
    normed = normed_rows(x_ref[...].reshape(rows * cols, chans))
    for i in range(rows):
        both = lax.dot_general(w_swap[...], normed[i * cols:(i + 1) * cols], NT, preferred_element_type=jnp.float32)
        gated = (jnp.tanh(both[:chans]) + 1.0) * both[chans:]
        row_mask = tok_s_ref[own_row + i].astype(jnp.float32)
        for h in range(cols // 128):
            swap[h, i * pitch:i * pitch + chans, :] = gated[:, h * 128:(h + 1) * 128] * (col_mask[h] * row_mask)
    for c in range(chans):
        for h in range(cols // 128):
            o_ref[c, :, h * 128:(h + 1) * 128] = swap[h, pl.ds(c, rows, stride=pitch), :].astype(jnp.bfloat16)


def project(pair, weight, token_mask, first, rows):
    cols, chans = pair.shape[1:]
    base = first // ROW_STEP
    return pl.pallas_call(
        functools.partial(project_kernel, first),
        grid=(rows // ROW_STEP,),
        in_specs=[
            pl.BlockSpec(memory_space=pltpu.SMEM),
            pl.BlockSpec((token_mask.shape[0] // 128, 128), lambda s: (0, 0)),
            pl.BlockSpec((ROW_STEP, cols, chans), lambda s: (base + s, 0, 0)),
            pl.BlockSpec((chans, 2 * chans), lambda s: (0, 0)),
        ],
        out_specs=pl.BlockSpec((chans, ROW_STEP, cols), lambda s: (0, s, 0)),
        out_shape=jax.ShapeDtypeStruct((chans, rows, cols), jnp.bfloat16),
        scratch_shapes=[
            pltpu.VMEM((2 * chans, chans), jnp.bfloat16),
            pltpu.VMEM((cols // 128, ROW_STEP * (chans + 1), 128), jnp.float32),
        ],
        compiler_params=pltpu.CompilerParams(vmem_limit_bytes=48 << 20),
    )(token_mask, token_mask.reshape(-1, 128), pair, weight)


def gate_kernel(x_ref, w_ref, o_ref):
    rows, blks, blk, chans = x_ref.shape
    normed = normed_rows(x_ref[...].reshape(rows * blks * blk, chans))
    gate = jnp.dot(normed, w_ref[...], preferred_element_type=jnp.float32)
    o_ref[...] = (0.5 * jnp.tanh(0.5 * gate) + 0.5).reshape(rows, blks * blk, chans).astype(jnp.bfloat16)


def gate_of(pair, w_gate):
    rows, cols, chans = pair.shape
    blks = cols // 128
    blocks = pair.reshape(rows, blks, 128, chans)
    return pl.pallas_call(
        gate_kernel,
        grid=(rows // 32,),
        in_specs=[
            pl.BlockSpec((32, blks, WIN_BLK, chans), lambda s: (s, 0, 0, 0)),
            pl.BlockSpec((chans, chans), lambda s: (0, 0)),
        ],
        out_specs=pl.BlockSpec((32, blks * WIN_BLK, chans), lambda s: (s, 0, 0)),
        out_shape=jax.ShapeDtypeStruct((rows, blks * WIN_BLK, chans), jnp.bfloat16),
        compiler_params=pltpu.CompilerParams(vmem_limit_bytes=48 << 20),
    )(blocks, w_gate)


def product_kernel(a_ref, b_ref, o_ref, acc):
    steps, parts, rows, depth = a_ref.shape
    wins, blk = b_ref.shape[0], b_ref.shape[2]
    half = rows // 2
    for q in range(parts):
        term = lax.dot_general(
            a_ref[:, q].reshape(steps * rows, depth), b_ref[:, q].reshape(wins * blk, depth), NT,
            preferred_element_type=jnp.float32)
        if q == 0:
            acc[...] = term
        else:
            acc[...] += term
    low = lax.broadcasted_iota(jnp.int32, (half, 128), 1) < 64
    for r in range(steps):
        for m in range(wins * blk // 128):
            top = acc[r * rows:r * rows + half, m * 128:(m + 1) * 128]
            bot = acc[r * rows + half:(r + 1) * rows, m * 128:(m + 1) * 128]
            o_ref[r, 2 * m] = jnp.where(low, top, pltpu.roll(bot, 64, 1)).astype(jnp.bfloat16)
            o_ref[r, 2 * m + 1] = jnp.where(low, pltpu.roll(top, 64, 1), bot).astype(jnp.bfloat16)


def product_of(left, right, n_row, n_chan):
    rows, depth = left.shape[1:]
    blk = right.shape[1]
    left = left.reshape(n_row, n_chan, rows, depth)
    right = right.reshape(n_row, n_chan, blk, depth)
    steps = 4
    out = pl.pallas_call(
        product_kernel,
        grid=(n_row // steps,),
        in_specs=[
            pl.BlockSpec((steps, n_chan, rows, depth), lambda s: (s, 0, 0, 0)),
            pl.BlockSpec((n_row, n_chan, blk, depth), lambda s: (0, 0, 0, 0)),
        ],
        out_specs=pl.BlockSpec((steps, n_chan, rows // 2, 128), lambda s: (s, 0, 0, 0)),
        out_shape=jax.ShapeDtypeStruct((n_row, n_chan, rows // 2, 128), jnp.bfloat16),
        scratch_shapes=[pltpu.VMEM((steps * rows, n_row * blk), jnp.float32)],
        compiler_params=pltpu.CompilerParams(vmem_limit_bytes=48 << 20),
    )(left, right)
    return out.reshape(n_row * n_chan, rows // 2, 128)


def finish_kernel(gain_ref, p_ref, w_ref, gate_ref, o_ref, swap):
    chans, subs, lanes = p_ref.shape
    pitch = subs + 1
    x = p_ref[...].astype(jnp.float32)
    mean = jnp.sum(x, axis=0) * (1.0 / chans)
    centred = x - mean[None]
    var = jnp.sum(centred * centred, axis=0) * (1.0 / chans)
    scale = lax.rsqrt(var + 1e-05)
    for c in range(chans):
        swap[c * pitch:c * pitch + subs, :] = centred[c] * scale * gain_ref[c]
    half = lanes // 2
    for s in range(subs):
        normed = swap[pl.ds(s, chans, stride=pitch), :].astype(jnp.bfloat16)
        outcome = lax.dot_general(normed, w_ref[...], TN, preferred_element_type=jnp.float32)
        for h in range(2):
            gate = gate_ref[h, s].astype(jnp.float32)
            o_ref[h, s] = (gate * outcome[h * half:(h + 1) * half]).astype(jnp.bfloat16)


def finish(product, out_gain, w_out, gate):
    chans, subs, lanes = product.shape
    rows, wins = gate.shape[:2]
    step = 16
    out = pl.pallas_call(
        finish_kernel,
        grid=(subs // step,),
        in_specs=[
            pl.BlockSpec(memory_space=pltpu.SMEM),
            pl.BlockSpec((chans, step, lanes), lambda s: (0, s, 0)),
            pl.BlockSpec((chans, chans), lambda s: (0, 0)),
            pl.BlockSpec((2, step, wins, chans), lambda s: (0, s, 0, 0)),
        ],
        out_specs=pl.BlockSpec((2, step, wins, chans), lambda s: (0, s, 0, 0)),
        out_shape=jax.ShapeDtypeStruct((2, subs, wins, chans), jnp.bfloat16),
        scratch_shapes=[pltpu.VMEM((chans * (step + 1), lanes), jnp.float32)],
        compiler_params=pltpu.CompilerParams(vmem_limit_bytes=48 << 20),
    )(out_gain, product, w_out, gate.reshape(2, subs, wins, chans))
    return out.reshape(rows, wins, chans)


def spread(values):
    return lax.all_to_all(values, AXES, split_axis=0, concat_axis=0, tiled=True)


def per_device(n_row, n_chan, pair, token_mask, w_left, w_right, w_gate, w_out, out_gain):
    right = spread(project(pair, w_right, token_mask, 0, WIN_BLK))
    left = spread(project(pair, w_left, token_mask, 0, pair.shape[0]))
    gate = gate_of(pair, w_gate)
    product = spread(product_of(left, right, n_row, n_chan))
    return finish(product, out_gain, w_out, gate)


def solution(mesh):
    in_specs = (P("row", "chan", None), P(), P(), P(), P(), P(), P())
    out_specs = P("row", "chan", None)
    body = functools.partial(per_device, mesh.shape["row"], mesh.shape["chan"])
    return jax.shard_map(
        body, mesh=mesh, in_specs=in_specs, out_specs=out_specs, check_vma=False
    )
```

```python
import jax
import jax.numpy as jnp
from jax import lax
from jax.experimental import pallas as pl
from jax.experimental.pallas import tpu as pltpu
from jax.sharding import PartitionSpec as P

TOK_ROW = 128
WIN_BLK = 32
ROW_STEP = 16
PROJECT_VMEM = 48 << 20
AXES = ("row", "chan")
NT = (((1,), (1,)), ((), ()))
TN = (((0,), (0,)), ((), ()))


def normed_rows(x):
    chans = x.shape[-1]
    avg = jnp.full((chans, chans), 1.0 / chans, jnp.bfloat16)
    mean = jnp.dot(x, avg, preferred_element_type=jnp.float32)
    centred = x.astype(jnp.float32) - mean
    var = jnp.dot((centred * centred).astype(jnp.bfloat16), avg, preferred_element_type=jnp.float32)
    return (centred * lax.rsqrt(var + 1e-05)).astype(jnp.bfloat16)


def project_kernel(x_ref, left_ref, right_ref, tok_ref, o_ref, weights, swap):
    rows, cols, chans = x_ref.shape
    pitch = chans + 1
    step = pl.program_id(0)
    wins = WIN_BLK // rows

    @pl.when(step == 0)
    def _():
        weights[:2 * chans] = (0.5 * left_ref[...].astype(jnp.float32)).T.astype(jnp.bfloat16)
        weights[2 * chans:] = (0.5 * right_ref[...].astype(jnp.float32)).T.astype(jnp.bfloat16)

    own_col = lax.axis_index("chan") * (cols // 128)
    mask = jnp.concatenate([tok_ref[pl.ds(own_col + h, 1), :] for h in range(cols // 128)], axis=1).astype(jnp.float32)

    def sides(count):
        for i in range(rows):
            x = x_ref[i].T.astype(jnp.float32)
            centred = x - jnp.mean(x, axis=0, keepdims=True)
            var = jnp.mean(centred * centred, axis=0, keepdims=True)
            normed = (centred * (lax.rsqrt(var + 1e-05) * mask)).astype(jnp.bfloat16)
            both = jnp.dot(weights[:2 * chans * count], normed, preferred_element_type=jnp.float32)
            for side in range(count):
                gate, value = both[2 * side * chans:(2 * side + 1) * chans], both[(2 * side + 1) * chans:2 * (side + 1) * chans]
                gated = (jnp.tanh(gate) + 1.0) * value
                for h in range(cols // 128):
                    swap[side, h, i * pitch:i * pitch + chans, :] = gated[:, h * 128:(h + 1) * 128]
        for side in range(count):
            at = pl.multiple_of(step * rows + (0 if side else WIN_BLK), rows)
            for c in range(chans):
                for h in range(cols // 128):
                    o_ref[c, pl.ds(at, rows), h * 128:(h + 1) * 128] = (
                        swap[side, h, pl.ds(c, rows, stride=pitch), :].astype(jnp.bfloat16))

    pl.when(step < wins)(lambda: sides(2))
    pl.when(step >= wins)(lambda: sides(1))


def project(pair, w_left, w_right, token_mask):
    rows, cols, chans = pair.shape
    tokens = token_mask.reshape(-1, 128)
    return pl.pallas_call(
        project_kernel,
        grid=(rows // ROW_STEP,),
        in_specs=[
            pl.BlockSpec((ROW_STEP, cols, chans), lambda s: (s, 0, 0)),
            pl.BlockSpec((chans, 2 * chans), lambda s: (0, 0)),
            pl.BlockSpec((chans, 2 * chans), lambda s: (0, 0)),
            pl.BlockSpec(tokens.shape, lambda s: (0, 0)),
        ],
        out_specs=pl.BlockSpec(memory_space=pltpu.VMEM),
        out_shape=pltpu.VMEM((chans, WIN_BLK + rows, cols), jnp.bfloat16),
        scratch_shapes=[
            pltpu.VMEM((4 * chans, chans), jnp.bfloat16),
            pltpu.VMEM((2, cols // 128, ROW_STEP * (chans + 1), 128), jnp.float32),
        ],
        compiler_params=pltpu.CompilerParams(vmem_limit_bytes=PROJECT_VMEM),
    )(pair, w_left, w_right, tokens)


def gate_kernel(tok_ref, x_ref, w_ref, o_ref, mask):
    rows, blks, blk, chans = x_ref.shape

    @pl.when(pl.program_id(0) == 0)
    def _():
        for h in range(blks):
            own_col = (lax.axis_index("chan") * blks + h) * 128
            for t in range(blk):
                mask[h * blk + t:h * blk + t + 1, :] = jnp.full((1, chans), tok_ref[own_col + t].astype(jnp.float32))

    own_row = lax.axis_index("row") * TOK_ROW + pl.program_id(0) * rows
    normed = normed_rows(x_ref[...].reshape(rows * blks * blk, chans))
    gate = jnp.dot(normed, w_ref[...], preferred_element_type=jnp.float32)
    gate = (0.5 * jnp.tanh(0.5 * gate) + 0.5).reshape(rows, blks * blk, chans)
    for i in range(rows):
        o_ref[i] = (gate[i] * (mask[...] * tok_ref[own_row + i].astype(jnp.float32))).astype(jnp.bfloat16)


def gate_of(pair, w_gate, token_mask):
    rows, cols, chans = pair.shape
    blks = cols // 128
    blocks = pair.reshape(rows, blks, 128, chans)
    return pl.pallas_call(
        gate_kernel,
        grid=(rows // 32,),
        in_specs=[
            pl.BlockSpec(memory_space=pltpu.SMEM),
            pl.BlockSpec((32, blks, WIN_BLK, chans), lambda s: (s, 0, 0, 0)),
            pl.BlockSpec((chans, chans), lambda s: (0, 0)),
        ],
        out_specs=pl.BlockSpec((None, 32, blks * WIN_BLK, chans), lambda s: (s // 2, s % 2, 0, 0)),
        out_shape=pltpu.HBM((2, rows // 2, blks * WIN_BLK, chans), jnp.bfloat16),
        scratch_shapes=[pltpu.VMEM((blks * WIN_BLK, chans), jnp.float32)],
        compiler_params=pltpu.CompilerParams(vmem_limit_bytes=20 << 20),
    )(token_mask, blocks, w_gate)


def product_kernel(x_ref, o_hbm, acc, out, sem):
    n_row, n_chan, rows, depth = x_ref.shape
    rows -= WIN_BLK
    wins = n_row * WIN_BLK
    steps = acc.shape[0] // rows
    half = rows // 2
    low = lax.broadcasted_iota(jnp.int32, (half, 128), 1) < 64
    copies = []
    for first in range(0, n_row, steps):
        for q in range(n_chan):
            term = lax.dot_general(
                x_ref[first:first + steps, q, WIN_BLK:].reshape(steps * rows, depth),
                x_ref[:, q, :WIN_BLK].reshape(wins, depth), NT, preferred_element_type=jnp.float32)
            if q == 0:
                acc[...] = term
            else:
                acc[...] += term
        for r in range(steps):
            for m in range(wins // 128):
                top = acc[r * rows:r * rows + half, m * 128:(m + 1) * 128]
                bot = acc[r * rows + half:(r + 1) * rows, m * 128:(m + 1) * 128]
                out[first + r, 2 * m] = jnp.where(low, top, pltpu.roll(bot, 64, 1)).astype(jnp.bfloat16)
                out[first + r, 2 * m + 1] = jnp.where(low, pltpu.roll(top, 64, 1), bot).astype(jnp.bfloat16)
        part = pl.ds(first, steps)
        copies.append(pltpu.make_async_copy(out.at[part], o_hbm.at[part], sem.at[first // steps]))
        copies[-1].start()
    for copy in copies:
        copy.wait()


def product_of(sides):
    n_row, n_chan = lax.axis_size("row"), lax.axis_size("chan")
    _, rows, depth = sides.shape
    half = (rows - WIN_BLK) // 2
    shape = (n_row, n_chan, half, 128)
    steps = 4
    out = pl.pallas_call(
        product_kernel,
        in_specs=[pl.BlockSpec(memory_space=pltpu.VMEM)],
        out_specs=pl.BlockSpec(memory_space=pltpu.HBM),
        out_shape=pltpu.HBM(shape, jnp.bfloat16),
        scratch_shapes=[
            pltpu.VMEM((steps * 2 * half, n_row * WIN_BLK), jnp.float32),
            pltpu.VMEM(shape, jnp.bfloat16),
            pltpu.SemaphoreType.DMA((n_row // steps,)),
        ],
        compiler_params=pltpu.CompilerParams(vmem_limit_bytes=16 << 20),
    )(sides.reshape(n_row, n_chan, rows, depth))
    return out.reshape(n_row * n_chan, half, 128)


def finish_kernel(gain_ref, p_ref, w_ref, gate_hbm, o_ref, swap, gate_ref, sem):
    chans, subs, lanes = p_ref.shape
    pitch = subs + 1
    half = lanes // 2
    step = pl.program_id(0)

    def gate_copy(n):
        part = pl.ds(pl.multiple_of(n * subs, subs), subs)
        return pltpu.make_async_copy(gate_hbm.at[:, part], gate_ref.at[n], sem.at[n])

    @pl.when(step == 0)
    def _():
        for n in range(gate_ref.shape[0]):
            gate_copy(n).start()

    x = p_ref[...].astype(jnp.float32)
    mean = jnp.sum(x, axis=0) * (1.0 / chans)
    centred = x - mean[None]
    var = jnp.sum(centred * centred, axis=0) * (1.0 / chans)
    scale = lax.rsqrt(var + 1e-05)
    for c in range(chans):
        swap[c * pitch:c * pitch + subs, :] = centred[c] * scale * gain_ref[c]
    gate_copy(step).wait()
    for s in range(subs):
        normed = swap[pl.ds(s, chans, stride=pitch), :].astype(jnp.bfloat16)
        outcome = lax.dot_general(normed, w_ref[...], TN, preferred_element_type=jnp.float32)
        for h in range(2):
            gate = gate_ref[step, h, s].astype(jnp.float32)
            o_ref[h, s] = (gate * outcome[h * half:(h + 1) * half]).astype(jnp.bfloat16)


def finish(product, out_gain, w_out, gate):
    chans, subs, lanes = product.shape
    rows, wins = 2 * subs, gate.shape[2]
    step = 16
    out = pl.pallas_call(
        finish_kernel,
        grid=(subs // step,),
        in_specs=[
            pl.BlockSpec(memory_space=pltpu.SMEM),
            pl.BlockSpec((chans, step, lanes), lambda s: (0, s, 0)),
            pl.BlockSpec((chans, chans), lambda s: (0, 0)),
            pl.BlockSpec(memory_space=pltpu.HBM),
        ],
        out_specs=pl.BlockSpec((2, step, wins, chans), lambda s: (0, s, 0, 0)),
        out_shape=pltpu.HBM((2, subs, wins, chans), jnp.bfloat16),
        scratch_shapes=[
            pltpu.VMEM((chans * (step + 1), lanes), jnp.float32),
            pltpu.VMEM((subs // step, 2, step, wins, chans), jnp.bfloat16),
            pltpu.SemaphoreType.DMA((subs // step,)),
        ],
        compiler_params=pltpu.CompilerParams(vmem_limit_bytes=60 << 20),
    )(out_gain, product, w_out, gate)
    return out.reshape(rows, wins, chans)


def spread(values):
    return lax.all_to_all(values, AXES, split_axis=0, concat_axis=0, tiled=True)


def per_device(pair, token_mask, w_left, w_right, w_gate, w_out, out_gain):
    sides = spread(project(pair, w_left, w_right, token_mask))
    gate = gate_of(pair, w_gate, token_mask)
    product = spread(product_of(sides))
    return finish(product, out_gain, w_out, gate)


def solution(mesh):
    in_specs = (P("row", "chan", None), P(), P(), P(), P(), P(), P())
    out_specs = P("row", "chan", None)
    return jax.shard_map(
        per_device, mesh=mesh, in_specs=in_specs, out_specs=out_specs, check_vma=False
    )
```

```python
import jax
import jax.numpy as jnp
from jax import lax
from jax.experimental import pallas as pl
from jax.experimental.pallas import tpu as pltpu
from jax.sharding import PartitionSpec as P

TOK_ROW = 128
WIN_BLK = 32
ROW_STEP = 16
FINISH_STEP = 16
PROJECT_VMEM = 48 << 20
AXES = ("row", "chan")
NT = (((1,), (1,)), ((), ()))
TN = (((0,), (0,)), ((), ()))


def normed_rows(x):
    chans = x.shape[-1]
    avg = jnp.full((chans, chans), 1.0 / chans, jnp.bfloat16)
    mean = jnp.dot(x, avg, preferred_element_type=jnp.float32)
    centred = x.astype(jnp.float32) - mean
    var = jnp.dot((centred * centred).astype(jnp.bfloat16), avg, preferred_element_type=jnp.float32)
    return (centred * lax.rsqrt(var + 1e-05)).astype(jnp.bfloat16)


def project_kernel(x_ref, left_ref, right_ref, tok_ref, o_ref, weights, swap):
    rows, cols, chans = x_ref.shape
    pitch = chans + 1
    step = pl.program_id(0)
    wins = WIN_BLK // rows

    @pl.when(step == 0)
    def _():
        weights[:2 * chans] = (0.5 * left_ref[...].astype(jnp.float32)).T.astype(jnp.bfloat16)
        weights[2 * chans:] = (0.5 * right_ref[...].astype(jnp.float32)).T.astype(jnp.bfloat16)

    own_col = lax.axis_index("chan") * (cols // 128)
    mask = jnp.concatenate([tok_ref[pl.ds(own_col + h, 1), :] for h in range(cols // 128)], axis=1).astype(jnp.float32)

    def sides(count):
        for i in range(rows):
            x = x_ref[i].T.astype(jnp.float32)
            centred = x - jnp.mean(x, axis=0, keepdims=True)
            var = jnp.mean(centred * centred, axis=0, keepdims=True)
            normed = (centred * (lax.rsqrt(var + 1e-05) * mask)).astype(jnp.bfloat16)
            both = jnp.dot(weights[:2 * chans * count], normed, preferred_element_type=jnp.float32)
            for side in range(count):
                gate, value = both[2 * side * chans:(2 * side + 1) * chans], both[(2 * side + 1) * chans:2 * (side + 1) * chans]
                gated = (jnp.tanh(gate) + 1.0) * value
                for h in range(cols // 128):
                    swap[side, h, i * pitch:i * pitch + chans, :] = gated[:, h * 128:(h + 1) * 128]
        for side in range(count):
            at = pl.multiple_of(step * rows + (0 if side else WIN_BLK), rows)
            for c in range(chans):
                for h in range(cols // 128):
                    o_ref[c, pl.ds(at, rows), h * 128:(h + 1) * 128] = (
                        swap[side, h, pl.ds(c, rows, stride=pitch), :].astype(jnp.bfloat16))

    pl.when(step < wins)(lambda: sides(2))
    pl.when(step >= wins)(lambda: sides(1))


def project(pair, w_left, w_right, token_mask):
    rows, cols, chans = pair.shape
    tokens = token_mask.reshape(-1, 128)
    return pl.pallas_call(
        project_kernel,
        grid=(rows // ROW_STEP,),
        in_specs=[
            pl.BlockSpec((ROW_STEP, cols, chans), lambda s: (s, 0, 0)),
            pl.BlockSpec((chans, 2 * chans), lambda s: (0, 0)),
            pl.BlockSpec((chans, 2 * chans), lambda s: (0, 0)),
            pl.BlockSpec(tokens.shape, lambda s: (0, 0)),
        ],
        out_specs=pl.BlockSpec(memory_space=pltpu.VMEM),
        out_shape=pltpu.VMEM((chans, WIN_BLK + rows, cols), jnp.bfloat16),
        scratch_shapes=[
            pltpu.VMEM((4 * chans, chans), jnp.bfloat16),
            pltpu.VMEM((2, cols // 128, ROW_STEP * (chans + 1), 128), jnp.float32),
        ],
        compiler_params=pltpu.CompilerParams(vmem_limit_bytes=PROJECT_VMEM),
    )(pair, w_left, w_right, tokens)


def gate_kernel(tok_ref, x_ref, w_ref, o_ref, mask):
    rows, blks, blk, chans = x_ref.shape

    @pl.when(pl.program_id(0) == 0)
    def _():
        for h in range(blks):
            own_col = (lax.axis_index("chan") * blks + h) * 128
            for t in range(blk):
                mask[h * blk + t:h * blk + t + 1, :] = jnp.full((1, chans), tok_ref[own_col + t].astype(jnp.float32))

    own_row = lax.axis_index("row") * TOK_ROW + pl.program_id(0) * rows
    normed = normed_rows(x_ref[...].reshape(rows * blks * blk, chans))
    gate = jnp.dot(normed, w_ref[...], preferred_element_type=jnp.float32)
    gate = (0.5 * jnp.tanh(0.5 * gate) + 0.5).reshape(rows, blks * blk, chans)
    for i in range(rows):
        o_ref[i] = (gate[i] * (mask[...] * tok_ref[own_row + i].astype(jnp.float32))).astype(jnp.bfloat16)


def gate_of(pair, w_gate, token_mask):
    rows, cols, chans = pair.shape
    blks = cols // 128
    blocks = pair.reshape(rows, blks, 128, chans)
    return pl.pallas_call(
        gate_kernel,
        grid=(rows // 32,),
        in_specs=[
            pl.BlockSpec(memory_space=pltpu.SMEM),
            pl.BlockSpec((32, blks, WIN_BLK, chans), lambda s: (s, 0, 0, 0)),
            pl.BlockSpec((chans, chans), lambda s: (0, 0)),
        ],
        out_specs=pl.BlockSpec((None, 32, blks * WIN_BLK, chans), lambda s: (s // 2, s % 2, 0, 0)),
        out_shape=pltpu.HBM((2, rows // 2, blks * WIN_BLK, chans), jnp.bfloat16),
        scratch_shapes=[pltpu.VMEM((blks * WIN_BLK, chans), jnp.float32)],
        compiler_params=pltpu.CompilerParams(vmem_limit_bytes=20 << 20),
    )(token_mask, blocks, w_gate)


def product_kernel(x_ref, o_hbm, acc, out, sem):
    n_row, n_chan, rows, depth = x_ref.shape
    rows -= WIN_BLK
    wins = n_row * WIN_BLK
    steps = acc.shape[0] // rows
    half = rows // 2
    low = lax.broadcasted_iota(jnp.int32, (half, 128), 1) < 64
    copies = []
    for first in range(0, n_row, steps):
        for q in range(n_chan):
            term = lax.dot_general(
                x_ref[first:first + steps, q, WIN_BLK:].reshape(steps * rows, depth),
                x_ref[:, q, :WIN_BLK].reshape(wins, depth), NT, preferred_element_type=jnp.float32)
            if q == 0:
                acc[...] = term
            else:
                acc[...] += term
        for r in range(steps):
            for m in range(wins // 128):
                top = acc[r * rows:r * rows + half, m * 128:(m + 1) * 128]
                bot = acc[r * rows + half:(r + 1) * rows, m * 128:(m + 1) * 128]
                out[first + r, 2 * m] = jnp.where(low, top, pltpu.roll(bot, 64, 1)).astype(jnp.bfloat16)
                out[first + r, 2 * m + 1] = jnp.where(low, pltpu.roll(top, 64, 1), bot).astype(jnp.bfloat16)
        part = pl.ds(first, steps)
        copies.append(pltpu.make_async_copy(out.at[part], o_hbm.at[part], sem.at[first // steps]))
        copies[-1].start()
    for copy in copies:
        copy.wait()


def product_of(sides):
    n_row, n_chan = lax.axis_size("row"), lax.axis_size("chan")
    _, rows, depth = sides.shape
    half = (rows - WIN_BLK) // 2
    shape = (n_row, n_chan, half, 128)
    steps = 4
    out = pl.pallas_call(
        product_kernel,
        in_specs=[pl.BlockSpec(memory_space=pltpu.VMEM)],
        out_specs=pl.BlockSpec(memory_space=pltpu.HBM),
        out_shape=pltpu.HBM(shape, jnp.bfloat16),
        scratch_shapes=[
            pltpu.VMEM((steps * 2 * half, n_row * WIN_BLK), jnp.float32),
            pltpu.VMEM(shape, jnp.bfloat16),
            pltpu.SemaphoreType.DMA((n_row // steps,)),
        ],
        compiler_params=pltpu.CompilerParams(vmem_limit_bytes=16 << 20),
    )(sides.reshape(n_row, n_chan, rows, depth))
    return out.reshape(n_row * n_chan, half, 128)


def finish_kernel(gain_ref, p_ref, w_ref, gate_hbm, o_hbm, swap, gate_ref, out, in_sem, out_sem):
    chans, subs, lanes = p_ref.shape
    half = lanes // 2
    parts = [pl.ds(first, FINISH_STEP) for first in range(0, subs, FINISH_STEP)]
    pitch = FINISH_STEP + 1
    gates = [
        pltpu.make_async_copy(gate_hbm.at[:, part], gate_ref.at[:, part], in_sem.at[n]) for n, part in enumerate(parts)]
    outs = [pltpu.make_async_copy(out.at[:, part], o_hbm.at[:, part], out_sem.at[n]) for n, part in enumerate(parts)]
    for copy in gates:
        copy.start()
    for n, part in enumerate(parts):
        x = p_ref[:, part].astype(jnp.float32)
        mean = jnp.sum(x, axis=0) * (1.0 / chans)
        centred = x - mean[None]
        var = jnp.sum(centred * centred, axis=0) * (1.0 / chans)
        scale = lax.rsqrt(var + 1e-05)
        for c in range(chans):
            swap[n % 2, c * pitch:c * pitch + FINISH_STEP, :] = centred[c] * scale * gain_ref[c]
        gates[n].wait()
        for s in range(FINISH_STEP):
            normed = swap[n % 2, pl.ds(s, chans, stride=pitch), :].astype(jnp.bfloat16)
            outcome = lax.dot_general(normed, w_ref[...], TN, preferred_element_type=jnp.float32)
            for h in range(2):
                gate = gate_ref[h, part.start + s].astype(jnp.float32)
                out[h, part.start + s] = (gate * outcome[h * half:(h + 1) * half]).astype(jnp.bfloat16)
        outs[n].start()
    for copy in outs:
        copy.wait()


def finish(product, out_gain, w_out, gate):
    chans, subs, lanes = product.shape
    out = pl.pallas_call(
        finish_kernel,
        in_specs=[
            pl.BlockSpec(memory_space=pltpu.SMEM),
            pl.BlockSpec(memory_space=pltpu.VMEM),
            pl.BlockSpec(memory_space=pltpu.VMEM),
            pl.BlockSpec(memory_space=pltpu.HBM),
        ],
        out_specs=pl.BlockSpec(memory_space=pltpu.HBM),
        out_shape=pltpu.HBM(gate.shape, jnp.bfloat16),
        scratch_shapes=[
            pltpu.VMEM((2, chans * (FINISH_STEP + 1), lanes), jnp.float32),
            pltpu.VMEM(gate.shape, jnp.bfloat16),
            pltpu.VMEM(gate.shape, jnp.bfloat16),
            pltpu.SemaphoreType.DMA((subs // FINISH_STEP,)),
            pltpu.SemaphoreType.DMA((subs // FINISH_STEP,)),
        ],
        compiler_params=pltpu.CompilerParams(vmem_limit_bytes=50 << 20),
    )(out_gain, product, w_out, gate)
    return out.reshape(2 * subs, gate.shape[2], chans)


def spread(values):
    return lax.all_to_all(values, AXES, split_axis=0, concat_axis=0, tiled=True)


def per_device(pair, token_mask, w_left, w_right, w_gate, w_out, out_gain):
    sides = spread(project(pair, w_left, w_right, token_mask))
    gate = gate_of(pair, w_gate, token_mask)
    product = spread(product_of(sides))
    return finish(product, out_gain, w_out, gate)


def solution(mesh):
    in_specs = (P("row", "chan", None), P(), P(), P(), P(), P(), P())
    out_specs = P("row", "chan", None)
    return jax.shard_map(
        per_device, mesh=mesh, in_specs=in_specs, out_specs=out_specs, check_vma=False
    )
```

```python
import jax
import jax.numpy as jnp
from jax import lax
from jax.experimental import pallas as pl
from jax.experimental.pallas import tpu as pltpu
from jax.sharding import PartitionSpec as P

TOK_ROW = 128
WIN_BLK = 32
ROW_STEP = 16
FINISH_STEP = 16
PROJECT_VMEM = 48 << 20
AXES = ("row", "chan")
NT = (((1,), (1,)), ((), ()))
TN = (((0,), (0,)), ((), ()))


def normed_rows(x):
    chans = x.shape[-1]
    avg = jnp.full((chans, chans), 1.0 / chans, jnp.bfloat16)
    mean = jnp.dot(x, avg, preferred_element_type=jnp.float32)
    centred = x.astype(jnp.float32) - mean
    var = jnp.dot((centred * centred).astype(jnp.bfloat16), avg, preferred_element_type=jnp.float32)
    return (centred * lax.rsqrt(var + 1e-05)).astype(jnp.bfloat16)


def project_kernel(x_ref, left_ref, right_ref, tok_ref, o_ref, weights, swap):
    rows, cols, chans = x_ref.shape
    pitch = chans + 1
    step = pl.program_id(0)
    wins = WIN_BLK // rows

    @pl.when(step == 0)
    def _():
        weights[:2 * chans] = (0.5 * left_ref[...].astype(jnp.float32)).T.astype(jnp.bfloat16)
        weights[2 * chans:] = (0.5 * right_ref[...].astype(jnp.float32)).T.astype(jnp.bfloat16)

    own_col = lax.axis_index("chan") * (cols // 128)
    mask = jnp.concatenate([tok_ref[pl.ds(own_col + h, 1), :] for h in range(cols // 128)], axis=1).astype(jnp.float32)

    def sides(count):
        for i in range(rows):
            x = x_ref[i].T.astype(jnp.float32)
            centred = x - jnp.mean(x, axis=0, keepdims=True)
            var = jnp.mean(centred * centred, axis=0, keepdims=True)
            normed = (centred * (lax.rsqrt(var + 1e-05) * mask)).astype(jnp.bfloat16)
            both = jnp.dot(weights[:2 * chans * count], normed, preferred_element_type=jnp.float32)
            for side in range(count):
                gate, value = both[2 * side * chans:(2 * side + 1) * chans], both[(2 * side + 1) * chans:2 * (side + 1) * chans]
                gated = (jnp.tanh(gate) + 1.0) * value
                for h in range(cols // 128):
                    swap[side, h, i * pitch:i * pitch + chans, :] = gated[:, h * 128:(h + 1) * 128]
        for side in range(count):
            at = pl.multiple_of(step * rows + (0 if side else WIN_BLK), rows)
            for c in range(chans):
                for h in range(cols // 128):
                    o_ref[c, pl.ds(at, rows), h * 128:(h + 1) * 128] = (
                        swap[side, h, pl.ds(c, rows, stride=pitch), :].astype(jnp.bfloat16))

    pl.when(step < wins)(lambda: sides(2))
    pl.when(step >= wins)(lambda: sides(1))


def project(pair, w_left, w_right, token_mask):
    rows, cols, chans = pair.shape
    tokens = token_mask.reshape(-1, 128)
    return pl.pallas_call(
        project_kernel,
        grid=(rows // ROW_STEP,),
        in_specs=[
            pl.BlockSpec((ROW_STEP, cols, chans), lambda s: (s, 0, 0)),
            pl.BlockSpec((chans, 2 * chans), lambda s: (0, 0)),
            pl.BlockSpec((chans, 2 * chans), lambda s: (0, 0)),
            pl.BlockSpec(tokens.shape, lambda s: (0, 0)),
        ],
        out_specs=pl.BlockSpec(memory_space=pltpu.VMEM),
        out_shape=pltpu.VMEM((chans, WIN_BLK + rows, cols), jnp.bfloat16),
        scratch_shapes=[
            pltpu.VMEM((4 * chans, chans), jnp.bfloat16),
            pltpu.VMEM((2, cols // 128, (ROW_STEP + 1) * (chans + 1), 128), jnp.float32),
        ],
        compiler_params=pltpu.CompilerParams(vmem_limit_bytes=PROJECT_VMEM),
    )(pair, w_left, w_right, tokens)


def gate_kernel(tok_ref, x_ref, w_ref, o_ref, mask):
    rows, blks, blk, chans = x_ref.shape

    @pl.when(pl.program_id(0) == 0)
    def _():
        for h in range(blks):
            own_col = (lax.axis_index("chan") * blks + h) * 128
            for t in range(blk):
                mask[h * blk + t:h * blk + t + 1, :] = jnp.full((1, chans), tok_ref[own_col + t].astype(jnp.float32))

    own_row = lax.axis_index("row") * TOK_ROW + pl.program_id(0) * rows
    normed = normed_rows(x_ref[...].reshape(rows * blks * blk, chans))
    gate = jnp.dot(normed, w_ref[...], preferred_element_type=jnp.float32)
    gate = (0.5 * jnp.tanh(0.5 * gate) + 0.5).reshape(rows, blks * blk, chans)
    for i in range(rows):
        o_ref[i] = (gate[i] * (mask[...] * tok_ref[own_row + i].astype(jnp.float32))).astype(jnp.bfloat16)


def gate_of(pair, w_gate, token_mask):
    rows, cols, chans = pair.shape
    blks = cols // 128
    blocks = pair.reshape(rows, blks, 128, chans)
    return pl.pallas_call(
        gate_kernel,
        grid=(rows // 32,),
        in_specs=[
            pl.BlockSpec(memory_space=pltpu.SMEM),
            pl.BlockSpec((32, blks, WIN_BLK, chans), lambda s: (s, 0, 0, 0)),
            pl.BlockSpec((chans, chans), lambda s: (0, 0)),
        ],
        out_specs=pl.BlockSpec((None, 32, blks * WIN_BLK, chans), lambda s: (s // 2, s % 2, 0, 0)),
        out_shape=pltpu.HBM((2, rows // 2, blks * WIN_BLK, chans), jnp.bfloat16),
        scratch_shapes=[pltpu.VMEM((blks * WIN_BLK, chans), jnp.float32)],
        compiler_params=pltpu.CompilerParams(vmem_limit_bytes=20 << 20),
    )(token_mask, blocks, w_gate)


def product_kernel(x_ref, o_hbm, acc, out, sem):
    n_row, n_chan, rows, depth = x_ref.shape
    rows -= WIN_BLK
    wins = n_row * WIN_BLK
    steps = acc.shape[0] // rows
    half = rows // 2
    low = lax.broadcasted_iota(jnp.int32, (half, 128), 1) < 64
    copies = []
    for first in range(0, n_row, steps):
        for q in range(n_chan):
            term = lax.dot_general(
                x_ref[first:first + steps, q, WIN_BLK:].reshape(steps * rows, depth),
                x_ref[:, q, :WIN_BLK].reshape(wins, depth), NT, preferred_element_type=jnp.float32)
            if q == 0:
                acc[...] = term
            else:
                acc[...] += term
        for r in range(steps):
            for m in range(wins // 128):
                top = acc[r * rows:r * rows + half, m * 128:(m + 1) * 128]
                bot = acc[r * rows + half:(r + 1) * rows, m * 128:(m + 1) * 128]
                out[first + r, 2 * m] = jnp.where(low, top, pltpu.roll(bot, 64, 1)).astype(jnp.bfloat16)
                out[first + r, 2 * m + 1] = jnp.where(low, pltpu.roll(top, 64, 1), bot).astype(jnp.bfloat16)
        part = pl.ds(first, steps)
        copies.append(pltpu.make_async_copy(out.at[part], o_hbm.at[part], sem.at[first // steps]))
        copies[-1].start()
    for copy in copies:
        copy.wait()


def product_of(sides):
    n_row, n_chan = lax.axis_size("row"), lax.axis_size("chan")
    _, rows, depth = sides.shape
    half = (rows - WIN_BLK) // 2
    shape = (n_row, n_chan, half, 128)
    steps = 4
    out = pl.pallas_call(
        product_kernel,
        in_specs=[pl.BlockSpec(memory_space=pltpu.VMEM)],
        out_specs=pl.BlockSpec(memory_space=pltpu.HBM),
        out_shape=pltpu.HBM(shape, jnp.bfloat16),
        scratch_shapes=[
            pltpu.VMEM((steps * 2 * half, n_row * WIN_BLK), jnp.float32),
            pltpu.VMEM(shape, jnp.bfloat16),
            pltpu.SemaphoreType.DMA((n_row // steps,)),
        ],
        compiler_params=pltpu.CompilerParams(vmem_limit_bytes=16 << 20),
    )(sides.reshape(n_row, n_chan, rows, depth))
    return out.reshape(n_row * n_chan, half, 128)


def finish_kernel(gain_ref, p_ref, w_ref, gate_hbm, o_hbm, swap, gate_ref, out, in_sem, out_sem):
    chans, subs, lanes = p_ref.shape
    half = lanes // 2
    parts = [pl.ds(first, FINISH_STEP) for first in range(0, subs, FINISH_STEP)]
    pitch = FINISH_STEP + 1
    gates = [
        pltpu.make_async_copy(gate_hbm.at[:, part], gate_ref.at[:, part], in_sem.at[n]) for n, part in enumerate(parts)]
    outs = [pltpu.make_async_copy(out.at[:, part], o_hbm.at[:, part], out_sem.at[n]) for n, part in enumerate(parts)]
    for copy in gates:
        copy.start()
    for n, part in enumerate(parts):
        x = p_ref[:, part].astype(jnp.float32)
        mean = jnp.sum(x, axis=0) * (1.0 / chans)
        centred = x - mean[None]
        var = jnp.sum(centred * centred, axis=0) * (1.0 / chans)
        scale = lax.rsqrt(var + 1e-05)
        for c in range(chans):
            swap[n % 2, c * pitch:c * pitch + FINISH_STEP, :] = centred[c] * scale * gain_ref[c]
        gates[n].wait()
        for s in range(FINISH_STEP):
            normed = swap[n % 2, pl.ds(s, chans, stride=pitch), :].astype(jnp.bfloat16)
            outcome = lax.dot_general(normed, w_ref[...], TN, preferred_element_type=jnp.float32)
            for h in range(2):
                gate = gate_ref[h, part.start + s].astype(jnp.float32)
                out[h, part.start + s] = (gate * outcome[h * half:(h + 1) * half]).astype(jnp.bfloat16)
        outs[n].start()
    for copy in outs:
        copy.wait()


def finish(product, out_gain, w_out, gate):
    chans, subs, lanes = product.shape
    out = pl.pallas_call(
        finish_kernel,
        in_specs=[
            pl.BlockSpec(memory_space=pltpu.SMEM),
            pl.BlockSpec(memory_space=pltpu.VMEM),
            pl.BlockSpec(memory_space=pltpu.VMEM),
            pl.BlockSpec(memory_space=pltpu.HBM),
        ],
        out_specs=pl.BlockSpec(memory_space=pltpu.HBM),
        out_shape=pltpu.HBM(gate.shape, jnp.bfloat16),
        scratch_shapes=[
            pltpu.VMEM((2, (chans + 1) * (FINISH_STEP + 1), lanes), jnp.float32),
            pltpu.VMEM(gate.shape, jnp.bfloat16),
            pltpu.VMEM(gate.shape, jnp.bfloat16),
            pltpu.SemaphoreType.DMA((subs // FINISH_STEP,)),
            pltpu.SemaphoreType.DMA((subs // FINISH_STEP,)),
        ],
        compiler_params=pltpu.CompilerParams(vmem_limit_bytes=50 << 20),
    )(out_gain, product, w_out, gate)
    return out.reshape(2 * subs, gate.shape[2], chans)


def spread(values):
    return lax.all_to_all(values, AXES, split_axis=0, concat_axis=0, tiled=True)


def per_device(pair, token_mask, w_left, w_right, w_gate, w_out, out_gain):
    sides = spread(project(pair, w_left, w_right, token_mask))
    gate = gate_of(pair, w_gate, token_mask)
    product = spread(product_of(sides))
    return finish(product, out_gain, w_out, gate)


def solution(mesh):
    in_specs = (P("row", "chan", None), P(), P(), P(), P(), P(), P())
    out_specs = P("row", "chan", None)
    return jax.shard_map(
        per_device, mesh=mesh, in_specs=in_specs, out_specs=out_specs, check_vma=False
    )
```

```python
import jax
import jax.numpy as jnp
from jax import lax
from jax.experimental import pallas as pl
from jax.experimental.pallas import tpu as pltpu
from jax.sharding import PartitionSpec as P

TOK_ROW = 128
WIN_BLK = 32
ROW_STEP = 16
FINISH_STEP = 16
SEND_STEP = 4
PROJECT_VMEM = 48 << 20
AXES = ("row", "chan")
NT = (((1,), (1,)), ((), ()))
TN = (((0,), (0,)), ((), ()))


def normed_rows(x):
    chans = x.shape[-1]
    avg = jnp.full((chans, chans), 1.0 / chans, jnp.bfloat16)
    mean = jnp.dot(x, avg, preferred_element_type=jnp.float32)
    centred = x.astype(jnp.float32) - mean
    var = jnp.dot((centred * centred).astype(jnp.bfloat16), avg, preferred_element_type=jnp.float32)
    return (centred * lax.rsqrt(var + 1e-05)).astype(jnp.bfloat16)


def project_kernel(x_ref, left_ref, right_ref, tok_ref, o_ref, weights, swap):
    rows, cols, chans = x_ref.shape
    pitch = chans + 1
    step = pl.program_id(0)
    wins = WIN_BLK // rows

    @pl.when(step == 0)
    def _():
        weights[:2 * chans] = (0.5 * left_ref[...].astype(jnp.float32)).T.astype(jnp.bfloat16)
        weights[2 * chans:] = (0.5 * right_ref[...].astype(jnp.float32)).T.astype(jnp.bfloat16)

    own_col = lax.axis_index("chan") * (cols // 128)
    mask = jnp.concatenate([tok_ref[pl.ds(own_col + h, 1), :] for h in range(cols // 128)], axis=1).astype(jnp.float32)

    def sides(count):
        for i in range(rows):
            x = x_ref[i].T.astype(jnp.float32)
            centred = x - jnp.mean(x, axis=0, keepdims=True)
            var = jnp.mean(centred * centred, axis=0, keepdims=True)
            normed = (centred * (lax.rsqrt(var + 1e-05) * mask)).astype(jnp.bfloat16)
            both = jnp.dot(weights[:2 * chans * count], normed, preferred_element_type=jnp.float32)
            for side in range(count):
                gate, value = both[2 * side * chans:(2 * side + 1) * chans], both[(2 * side + 1) * chans:2 * (side + 1) * chans]
                gated = (jnp.tanh(gate) + 1.0) * value
                for h in range(cols // 128):
                    swap[side, h, i * pitch:i * pitch + chans, :] = gated[:, h * 128:(h + 1) * 128]
        for side in range(count):
            at = pl.multiple_of(step * rows + (0 if side else WIN_BLK), rows)
            for c in range(chans):
                for h in range(cols // 128):
                    o_ref[c, pl.ds(at, rows), h * 128:(h + 1) * 128] = (
                        swap[side, h, pl.ds(c, rows, stride=pitch), :].astype(jnp.bfloat16))

    pl.when(step < wins)(lambda: sides(2))
    pl.when(step >= wins)(lambda: sides(1))


def project(pair, w_left, w_right, token_mask):
    rows, cols, chans = pair.shape
    tokens = token_mask.reshape(-1, 128)
    return pl.pallas_call(
        project_kernel,
        grid=(rows // ROW_STEP,),
        in_specs=[
            pl.BlockSpec((ROW_STEP, cols, chans), lambda s: (s, 0, 0)),
            pl.BlockSpec((chans, 2 * chans), lambda s: (0, 0)),
            pl.BlockSpec((chans, 2 * chans), lambda s: (0, 0)),
            pl.BlockSpec(tokens.shape, lambda s: (0, 0)),
        ],
        out_specs=pl.BlockSpec(memory_space=pltpu.VMEM),
        out_shape=pltpu.VMEM((chans, WIN_BLK + rows, cols), jnp.bfloat16),
        scratch_shapes=[
            pltpu.VMEM((4 * chans, chans), jnp.bfloat16),
            pltpu.VMEM((2, cols // 128, (ROW_STEP + 1) * (chans + 1), 128), jnp.float32),
        ],
        compiler_params=pltpu.CompilerParams(vmem_limit_bytes=PROJECT_VMEM),
    )(pair, w_left, w_right, tokens)


def gate_kernel(tok_ref, x_ref, w_ref, o_ref, mask):
    rows, blks, blk, chans = x_ref.shape

    @pl.when(pl.program_id(0) == 0)
    def _():
        for h in range(blks):
            own_col = (lax.axis_index("chan") * blks + h) * 128
            for t in range(blk):
                mask[h * blk + t:h * blk + t + 1, :] = jnp.full((1, chans), tok_ref[own_col + t].astype(jnp.float32))

    own_row = lax.axis_index("row") * TOK_ROW + pl.program_id(0) * rows
    normed = normed_rows(x_ref[...].reshape(rows * blks * blk, chans))
    gate = jnp.dot(normed, w_ref[...], preferred_element_type=jnp.float32)
    gate = (0.5 * jnp.tanh(0.5 * gate) + 0.5).reshape(rows, blks * blk, chans)
    for i in range(rows):
        o_ref[i] = (gate[i] * (mask[...] * tok_ref[own_row + i].astype(jnp.float32))).astype(jnp.bfloat16)


def gate_of(pair, w_gate, token_mask):
    rows, cols, chans = pair.shape
    blks = cols // 128
    blocks = pair.reshape(rows, blks, 128, chans)
    return pl.pallas_call(
        gate_kernel,
        grid=(rows // 32,),
        in_specs=[
            pl.BlockSpec(memory_space=pltpu.SMEM),
            pl.BlockSpec((32, blks, WIN_BLK, chans), lambda s: (s, 0, 0, 0)),
            pl.BlockSpec((chans, chans), lambda s: (0, 0)),
        ],
        out_specs=pl.BlockSpec((None, 32, blks * WIN_BLK, chans), lambda s: (s // 2, s % 2, 0, 0)),
        out_shape=pltpu.HBM((2, rows // 2, blks * WIN_BLK, chans), jnp.bfloat16),
        scratch_shapes=[pltpu.VMEM((blks * WIN_BLK, chans), jnp.float32)],
        compiler_params=pltpu.CompilerParams(vmem_limit_bytes=20 << 20),
    )(token_mask, blocks, w_gate)


def product_kernel(x_ref, o_hbm, acc, out, sem):
    n_row, n_chan, rows, depth = x_ref.shape
    rows -= WIN_BLK
    wins = n_row * WIN_BLK
    steps = acc.shape[0] // rows
    half = rows // 2
    low = lax.broadcasted_iota(jnp.int32, (half, 128), 1) < 64
    copies = []
    for first in range(0, n_row, steps):
        for q in range(n_chan):
            term = lax.dot_general(
                x_ref[first:first + steps, q, WIN_BLK:].reshape(steps * rows, depth),
                x_ref[:, q, :WIN_BLK].reshape(wins, depth), NT, preferred_element_type=jnp.float32)
            if q == 0:
                acc[...] = term
            else:
                acc[...] += term
        for r in range(steps):
            for m in range(wins // 128):
                top = acc[r * rows:r * rows + half, m * 128:(m + 1) * 128]
                bot = acc[r * rows + half:(r + 1) * rows, m * 128:(m + 1) * 128]
                out[first + r, 2 * m] = jnp.where(low, top, pltpu.roll(bot, 64, 1)).astype(jnp.bfloat16)
                out[first + r, 2 * m + 1] = jnp.where(low, pltpu.roll(top, 64, 1), bot).astype(jnp.bfloat16)
            copies.append(pltpu.make_async_copy(out.at[first + r], o_hbm.at[first + r], sem.at[first + r]))
            copies[-1].start()
    for copy in copies:
        copy.wait()


def product_of(sides):
    n_row, n_chan = lax.axis_size("row"), lax.axis_size("chan")
    _, rows, depth = sides.shape
    half = (rows - WIN_BLK) // 2
    shape = (n_row, n_chan, half, 128)
    steps = 4
    out = pl.pallas_call(
        product_kernel,
        in_specs=[pl.BlockSpec(memory_space=pltpu.VMEM)],
        out_specs=pl.BlockSpec(memory_space=pltpu.HBM),
        out_shape=pltpu.HBM(shape, jnp.bfloat16),
        scratch_shapes=[
            pltpu.VMEM((steps * 2 * half, n_row * WIN_BLK), jnp.float32),
            pltpu.VMEM(shape, jnp.bfloat16),
            pltpu.SemaphoreType.DMA((n_row,)),
        ],
        compiler_params=pltpu.CompilerParams(vmem_limit_bytes=16 << 20),
    )(sides.reshape(n_row, n_chan, rows, depth))
    return out.reshape(n_row * n_chan, half, 128)


def finish_kernel(gain_ref, p_ref, w_ref, gate_hbm, o_hbm, swap, gate_ref, out, in_sem, out_sem):
    chans, subs, lanes = p_ref.shape
    half = lanes // 2
    parts = [pl.ds(first, FINISH_STEP) for first in range(0, subs, FINISH_STEP)]
    pitch = FINISH_STEP + 1
    gates = [
        pltpu.make_async_copy(gate_hbm.at[:, part], gate_ref.at[:, part], in_sem.at[n]) for n, part in enumerate(parts)]
    sends = [pl.ds(first, SEND_STEP) for first in range(0, subs, SEND_STEP)]
    outs = [pltpu.make_async_copy(out.at[:, part], o_hbm.at[:, part], out_sem.at[n]) for n, part in enumerate(sends)]
    for copy in gates:
        copy.start()
    for n, part in enumerate(parts):
        x = p_ref[:, part].astype(jnp.float32)
        mean = jnp.sum(x, axis=0) * (1.0 / chans)
        centred = x - mean[None]
        var = jnp.sum(centred * centred, axis=0) * (1.0 / chans)
        scale = lax.rsqrt(var + 1e-05)
        for c in range(chans):
            swap[n % 2, c * pitch:c * pitch + FINISH_STEP, :] = centred[c] * scale * gain_ref[c]
        gates[n].wait()
        for s in range(FINISH_STEP):
            normed = swap[n % 2, pl.ds(s, chans, stride=pitch), :].astype(jnp.bfloat16)
            outcome = lax.dot_general(normed, w_ref[...], TN, preferred_element_type=jnp.float32)
            for h in range(2):
                gate = gate_ref[h, part.start + s].astype(jnp.float32)
                out[h, part.start + s] = (gate * outcome[h * half:(h + 1) * half]).astype(jnp.bfloat16)
            if (s + 1) % SEND_STEP == 0:
                outs[(part.start + s) // SEND_STEP].start()
    for copy in outs:
        copy.wait()


def finish(product, out_gain, w_out, gate):
    chans, subs, lanes = product.shape
    out = pl.pallas_call(
        finish_kernel,
        in_specs=[
            pl.BlockSpec(memory_space=pltpu.SMEM),
            pl.BlockSpec(memory_space=pltpu.VMEM),
            pl.BlockSpec(memory_space=pltpu.VMEM),
            pl.BlockSpec(memory_space=pltpu.HBM),
        ],
        out_specs=pl.BlockSpec(memory_space=pltpu.HBM),
        out_shape=pltpu.HBM(gate.shape, jnp.bfloat16),
        scratch_shapes=[
            pltpu.VMEM((2, (chans + 1) * (FINISH_STEP + 1), lanes), jnp.float32),
            pltpu.VMEM(gate.shape, jnp.bfloat16),
            pltpu.VMEM(gate.shape, jnp.bfloat16),
            pltpu.SemaphoreType.DMA((subs // FINISH_STEP,)),
            pltpu.SemaphoreType.DMA((subs // SEND_STEP,)),
        ],
        compiler_params=pltpu.CompilerParams(vmem_limit_bytes=50 << 20),
    )(out_gain, product, w_out, gate)
    return out.reshape(2 * subs, gate.shape[2], chans)


def spread(values):
    return lax.all_to_all(values, AXES, split_axis=0, concat_axis=0, tiled=True)


def per_device(pair, token_mask, w_left, w_right, w_gate, w_out, out_gain):
    sides = spread(project(pair, w_left, w_right, token_mask))
    gate = gate_of(pair, w_gate, token_mask)
    product = spread(product_of(sides))
    return finish(product, out_gain, w_out, gate)


def solution(mesh):
    in_specs = (P("row", "chan", None), P(), P(), P(), P(), P(), P())
    out_specs = P("row", "chan", None)
    return jax.shard_map(
        per_device, mesh=mesh, in_specs=in_specs, out_specs=out_specs, check_vma=False
    )
```

```python
import jax
import jax.numpy as jnp
from jax import lax
from jax.experimental import pallas as pl
from jax.experimental.pallas import tpu as pltpu
from jax.sharding import PartitionSpec as P

TOK_ROW = 128
WIN_BLK = 32
ROW_STEP = 16
FINISH_STEP = 16
PROJECT_VMEM = 48 << 20
AXES = ("row", "chan")
NT = (((1,), (1,)), ((), ()))
TN = (((0,), (0,)), ((), ()))


def normed_rows(x):
    chans = x.shape[-1]
    avg = jnp.full((chans, chans), 1.0 / chans, jnp.bfloat16)
    mean = jnp.dot(x, avg, preferred_element_type=jnp.float32)
    centred = x.astype(jnp.float32) - mean
    var = jnp.dot((centred * centred).astype(jnp.bfloat16), avg, preferred_element_type=jnp.float32)
    return (centred * lax.rsqrt(var + 1e-05)).astype(jnp.bfloat16)


def project_kernel(x_ref, left_ref, right_ref, tok_ref, o_ref, weights, swap):
    rows, cols, chans = x_ref.shape
    pitch = chans + 1
    step = pl.program_id(0)
    wins = WIN_BLK // rows

    @pl.when(step == 0)
    def _():
        weights[:2 * chans] = (0.5 * left_ref[...].astype(jnp.float32)).T.astype(jnp.bfloat16)
        weights[2 * chans:] = (0.5 * right_ref[...].astype(jnp.float32)).T.astype(jnp.bfloat16)

    own_col = lax.axis_index("chan") * (cols // 128)
    mask = jnp.concatenate([tok_ref[pl.ds(own_col + h, 1), :] for h in range(cols // 128)], axis=1).astype(jnp.float32)

    def sides(count):
        for i in range(rows):
            x = x_ref[i].T.astype(jnp.float32)
            centred = x - jnp.mean(x, axis=0, keepdims=True)
            var = jnp.mean(centred * centred, axis=0, keepdims=True)
            normed = (centred * (lax.rsqrt(var + 1e-05) * mask)).astype(jnp.bfloat16)
            both = jnp.dot(weights[:2 * chans * count], normed, preferred_element_type=jnp.float32)
            for side in range(count):
                gate, value = both[2 * side * chans:(2 * side + 1) * chans], both[(2 * side + 1) * chans:2 * (side + 1) * chans]
                gated = (jnp.tanh(gate) + 1.0) * value
                for h in range(cols // 128):
                    swap[side, h, i * pitch:i * pitch + chans, :] = gated[:, h * 128:(h + 1) * 128]
        for side in range(count):
            at = pl.multiple_of(step * rows + (0 if side else WIN_BLK), rows)
            for c in range(chans):
                for h in range(cols // 128):
                    o_ref[c, pl.ds(at, rows), h * 128:(h + 1) * 128] = (
                        swap[side, h, pl.ds(c, rows, stride=pitch), :].astype(jnp.bfloat16))

    pl.when(step < wins)(lambda: sides(2))
    pl.when(step >= wins)(lambda: sides(1))


def project(pair, w_left, w_right, token_mask):
    rows, cols, chans = pair.shape
    tokens = token_mask.reshape(-1, 128)
    return pl.pallas_call(
        project_kernel,
        grid=(rows // ROW_STEP,),
        in_specs=[
            pl.BlockSpec((ROW_STEP, cols, chans), lambda s: (s, 0, 0)),
            pl.BlockSpec((chans, 2 * chans), lambda s: (0, 0)),
            pl.BlockSpec((chans, 2 * chans), lambda s: (0, 0)),
            pl.BlockSpec(tokens.shape, lambda s: (0, 0)),
        ],
        out_specs=pl.BlockSpec(memory_space=pltpu.VMEM),
        out_shape=pltpu.VMEM((chans, WIN_BLK + rows, cols), jnp.bfloat16),
        scratch_shapes=[
            pltpu.VMEM((4 * chans, chans), jnp.bfloat16),
            pltpu.VMEM((2, cols // 128, (ROW_STEP + 1) * (chans + 1), 128), jnp.float32),
        ],
        compiler_params=pltpu.CompilerParams(vmem_limit_bytes=PROJECT_VMEM),
    )(pair, w_left, w_right, tokens)


def gate_kernel(tok_ref, x_ref, w_ref, o_ref, mask):
    rows, blks, blk, chans = x_ref.shape

    @pl.when(pl.program_id(0) == 0)
    def _():
        for h in range(blks):
            own_col = (lax.axis_index("chan") * blks + h) * 128
            for t in range(blk):
                mask[h * blk + t:h * blk + t + 1, :] = jnp.full((1, chans), tok_ref[own_col + t].astype(jnp.float32))

    own_row = lax.axis_index("row") * TOK_ROW + pl.program_id(0) * rows
    normed = normed_rows(x_ref[...].reshape(rows * blks * blk, chans))
    gate = jnp.dot(normed, w_ref[...], preferred_element_type=jnp.float32)
    gate = (0.5 * jnp.tanh(0.5 * gate) + 0.5).reshape(rows, blks * blk, chans)
    for i in range(rows):
        o_ref[i] = (gate[i] * (mask[...] * tok_ref[own_row + i].astype(jnp.float32))).astype(jnp.bfloat16)


def gate_of(pair, w_gate, token_mask):
    rows, cols, chans = pair.shape
    blks = cols // 128
    blocks = pair.reshape(rows, blks, 128, chans)
    return pl.pallas_call(
        gate_kernel,
        grid=(rows // 32,),
        in_specs=[
            pl.BlockSpec(memory_space=pltpu.SMEM),
            pl.BlockSpec((32, blks, WIN_BLK, chans), lambda s: (s, 0, 0, 0)),
            pl.BlockSpec((chans, chans), lambda s: (0, 0)),
        ],
        out_specs=pl.BlockSpec((None, 32, blks * WIN_BLK, chans), lambda s: (s // 2, s % 2, 0, 0)),
        out_shape=pltpu.HBM((2, rows // 2, blks * WIN_BLK, chans), jnp.bfloat16),
        scratch_shapes=[pltpu.VMEM((blks * WIN_BLK, chans), jnp.float32)],
        compiler_params=pltpu.CompilerParams(vmem_limit_bytes=20 << 20),
    )(token_mask, blocks, w_gate)


def product_kernel(x_ref, o_hbm, acc, out, sem):
    n_row, n_chan, rows, depth = x_ref.shape
    rows -= WIN_BLK
    wins = n_row * WIN_BLK
    steps = acc.shape[0] // rows
    half = rows // 2
    low = lax.broadcasted_iota(jnp.int32, (half, 128), 1) < 64
    copies = []
    for first in range(0, n_row, steps):
        left = [x_ref[first:first + steps, q, WIN_BLK:].reshape(steps * rows, depth) for q in range(n_chan)]
        right = [x_ref[:, q, :WIN_BLK].reshape(wins, depth) for q in range(n_chan)]
        acc[...] = lax.dot_general(
            jnp.concatenate(left, axis=1), jnp.concatenate(right, axis=1), NT, preferred_element_type=jnp.float32)
        for r in range(steps):
            for m in range(wins // 128):
                top = acc[r * rows:r * rows + half, m * 128:(m + 1) * 128]
                bot = acc[r * rows + half:(r + 1) * rows, m * 128:(m + 1) * 128]
                out[first + r, 2 * m] = jnp.where(low, top, pltpu.roll(bot, 64, 1)).astype(jnp.bfloat16)
                out[first + r, 2 * m + 1] = jnp.where(low, pltpu.roll(top, 64, 1), bot).astype(jnp.bfloat16)
        part = pl.ds(first, steps)
        copies.append(pltpu.make_async_copy(out.at[part], o_hbm.at[part], sem.at[first // steps]))
        copies[-1].start()
    for copy in copies:
        copy.wait()


def product_of(sides):
    n_row, n_chan = lax.axis_size("row"), lax.axis_size("chan")
    _, rows, depth = sides.shape
    half = (rows - WIN_BLK) // 2
    shape = (n_row, n_chan, half, 128)
    steps = 4
    out = pl.pallas_call(
        product_kernel,
        in_specs=[pl.BlockSpec(memory_space=pltpu.VMEM)],
        out_specs=pl.BlockSpec(memory_space=pltpu.HBM),
        out_shape=pltpu.HBM(shape, jnp.bfloat16),
        scratch_shapes=[
            pltpu.VMEM((steps * 2 * half, n_row * WIN_BLK), jnp.float32),
            pltpu.VMEM(shape, jnp.bfloat16),
            pltpu.SemaphoreType.DMA((n_row // steps,)),
        ],
        compiler_params=pltpu.CompilerParams(vmem_limit_bytes=16 << 20),
    )(sides.reshape(n_row, n_chan, rows, depth))
    return out.reshape(n_row * n_chan, half, 128)


def finish_kernel(gain_ref, p_ref, w_ref, gate_hbm, o_hbm, swap, gate_ref, out, in_sem, out_sem):
    chans, subs, lanes = p_ref.shape
    half = lanes // 2
    parts = [pl.ds(first, FINISH_STEP) for first in range(0, subs, FINISH_STEP)]
    pitch = FINISH_STEP + 1
    gates = [
        pltpu.make_async_copy(gate_hbm.at[:, part], gate_ref.at[:, part], in_sem.at[n]) for n, part in enumerate(parts)]
    outs = [pltpu.make_async_copy(out.at[:, part], o_hbm.at[:, part], out_sem.at[n]) for n, part in enumerate(parts)]
    for copy in gates:
        copy.start()
    for n, part in enumerate(parts):
        x = p_ref[:, part].astype(jnp.float32)
        mean = jnp.sum(x, axis=0) * (1.0 / chans)
        centred = x - mean[None]
        var = jnp.sum(centred * centred, axis=0) * (1.0 / chans)
        scale = lax.rsqrt(var + 1e-05)
        for c in range(chans):
            swap[n % 2, c * pitch:c * pitch + FINISH_STEP, :] = centred[c] * scale * gain_ref[c]
        gates[n].wait()
        for s in range(FINISH_STEP):
            normed = swap[n % 2, pl.ds(s, chans, stride=pitch), :].astype(jnp.bfloat16)
            outcome = lax.dot_general(normed, w_ref[...], TN, preferred_element_type=jnp.float32)
            for h in range(2):
                gate = gate_ref[h, part.start + s].astype(jnp.float32)
                out[h, part.start + s] = (gate * outcome[h * half:(h + 1) * half]).astype(jnp.bfloat16)
        outs[n].start()
    for copy in outs:
        copy.wait()


def finish(product, out_gain, w_out, gate):
    chans, subs, lanes = product.shape
    out = pl.pallas_call(
        finish_kernel,
        in_specs=[
            pl.BlockSpec(memory_space=pltpu.SMEM),
            pl.BlockSpec(memory_space=pltpu.VMEM),
            pl.BlockSpec(memory_space=pltpu.VMEM),
            pl.BlockSpec(memory_space=pltpu.HBM),
        ],
        out_specs=pl.BlockSpec(memory_space=pltpu.HBM),
        out_shape=pltpu.HBM(gate.shape, jnp.bfloat16),
        scratch_shapes=[
            pltpu.VMEM((2, (chans + 1) * (FINISH_STEP + 1), lanes), jnp.float32),
            pltpu.VMEM(gate.shape, jnp.bfloat16),
            pltpu.VMEM(gate.shape, jnp.bfloat16),
            pltpu.SemaphoreType.DMA((subs // FINISH_STEP,)),
            pltpu.SemaphoreType.DMA((subs // FINISH_STEP,)),
        ],
        compiler_params=pltpu.CompilerParams(vmem_limit_bytes=50 << 20),
    )(out_gain, product, w_out, gate)
    return out.reshape(2 * subs, gate.shape[2], chans)


def spread(values):
    return lax.all_to_all(values, AXES, split_axis=0, concat_axis=0, tiled=True)


def per_device(pair, token_mask, w_left, w_right, w_gate, w_out, out_gain):
    sides = spread(project(pair, w_left, w_right, token_mask))
    gate = gate_of(pair, w_gate, token_mask)
    product = spread(product_of(sides))
    return finish(product, out_gain, w_out, gate)


def solution(mesh):
    in_specs = (P("row", "chan", None), P(), P(), P(), P(), P(), P())
    out_specs = P("row", "chan", None)
    return jax.shard_map(
        per_device, mesh=mesh, in_specs=in_specs, out_specs=out_specs, check_vma=False
    )
```
